32 devices in a mesh: dp: 8 (over z, x), expert: 4 (over y, core).
Axes of the slice: x: 2, y: 2, z: 4, core: 2. Of those that a mesh axis runs over, the one named last changes fastest.
Arguments:
- tokens: bfloat16 [4096, 1280], P(('dp', 'expert')), may hold values from -6 to 6
- routes: int32 [4096, 2], P(('dp', 'expert')), may hold values from 0 to 31, all different within a row; in each aligned block of 128 rows (0 to 127, 128 to 255, ...) at most 10 rows name the same one
- combine: float32 [4096, 2], P(('dp', 'expert')), may hold values from 0.1 to 1
- w_in: bfloat16 [1280, 163840], P(None, ('dp', 'expert')), may hold values from -0.15625 to 0.15625
- w_out: bfloat16 [163840, 1280], P(('dp', 'expert')), may hold values from -0.078125 to 0.078125
- out_grad: bfloat16 [4096, 1280], P(('dp', 'expert')), may hold values from -6 to 6
- head_w: bfloat16 [1280, 17408], P(None, 'expert'), may hold values from -0.5 to 0.5
- labels: int32 [16, 4], P('dp'), may hold values from 0 to 17407
Outputs:
- mixed_out: bfloat16 [4096, 1280], P(('dp', 'expert'))
- d_tokens: bfloat16 [4096, 1280], P(('dp', 'expert'))
- d_combine: float32 [4096, 2], P(('dp', 'expert'))
- d_w_in: bfloat16 [1280, 163840], P(None, ('dp', 'expert'))
- d_w_out: bfloat16 [163840, 1280], P(('dp', 'expert'))
- image_loss: float32 [16], P('dp')
- d_pooled: float32 [16, 1280], P('dp')
- d_head: bfloat16 [1280, 17408], P('dp', 'expert')
The draws below stay inside these ranges and needn't reach their ends.
Inputs may be any that keep to these rules, and one draw needn't show every extreme that they name: `routes`: in the 128 rows of each device no expert is named by more than 10 rows, a bound that some block reaches; the two entries of a row differ. `labels`: entries of one image may repeat.
All inputs are finite; a program needn't handle non-finite values.
Results may differ from the reference program's by a relative error of at most 0.015.
Values may be sent and summed in bfloat16 or wider, within the bound.
A program may use at most 192 MiB of HBM per device.

```python
import math
import jax
import jax.numpy as jnp
import numpy as np
from jax import lax

D = 1280
FF = 5120
EXPERTS = 32
PATCHES = 256
CLASSES = 17408
LAB = 4
TOK_DEV = 128
CAP = 10
TOKENS = 4096
IMAGES = 16
N_DP = 8
N_EXPERT = 4


def with_ends(array, key, low, top_value):
    dims = array.shape
    index_at = [jax.random.randint(jax.random.fold_in(key, axis), (), 0, dims[axis]) for axis in range(len(dims))]
    array = array.at[tuple(index_at)].set(low)
    longest = dims.index(max(dims))
    index_at[longest] = (index_at[longest] + 1) % dims[longest]
    return array.at[tuple(index_at)].set(top_value)


def steps_of(own_key, dims, pieces, low, top_value):
    def one(dim, blocks):
        heights = jax.random.uniform(jax.random.fold_in(jax.random.fold_in(own_key, 6), dim), (blocks,), jnp.float32, low / len(pieces), top_value / len(pieces))
        return jnp.repeat(jnp.exp(heights), dims[dim] // blocks).reshape((-1,) + (1,) * (len(dims) - dim - 1))

    loudness = one(*pieces[0])
    for cut in pieces[1:]:
        loudness = loudness * one(*cut)
    return loudness


def rank_table(count, skew):
    loads = [(1 << 20) // math.isqrt(standing ** skew) + 1 for standing in range(1, count + 1)]
    deviation = 1 + sum(loads) // (1 << 30)
    return np.cumsum(np.array([max(1, weight // deviation) for weight in loads]))


def ranked_ids(own_key, extent, count, skew):
    listing = rank_table(count, skew)
    lot = jax.random.randint(jax.random.fold_in(own_key, 1), extent, 0, int(listing[count - 1]))
    rank = jnp.searchsorted(jnp.asarray(listing, jnp.int32), lot, side="right")
    return jax.random.permutation(jax.random.fold_in(own_key, 2), count)[rank].astype(jnp.int32)


def routed_block(stream_key, own, number, rows, count, top, reach, slope):
    order = jax.random.permutation(stream_key, count)
    heavy_load, common = portions_of(count, rows * top, reach, slope, True), portions_of(count, rows * top, reach, slope, False)
    places = jnp.arange(count)

    def named(tallies, rotation):
        used = int((tallies > 0).sum())
        fixed = max(1, used // 4)
        shifted = fixed + (places - fixed + rotation * (used - fixed)) % max(1, count - fixed)
        return jnp.zeros((count,), jnp.int32).at[order[jnp.where(places < fixed, places, shifted)]].set(jnp.asarray(tallies, jnp.int32))

    tallies = jnp.where(number % 4 == 0, named(heavy_load, number // 4), named(common, number - number // 4 - 1))
    mixed = jax.random.permutation(jax.random.fold_in(own, 3), count)
    giver, sink = mixed[0:count // 2 * 2:2], mixed[1:count // 2 * 2:2]
    room = jnp.minimum(tallies[giver] - 1, reach - tallies[sink]) // 2
    room = jnp.where((giver == order[0]) | (sink == order[0]) | (tallies[sink] == 0), 0, jnp.maximum(room, 0))
    shifted = jax.random.randint(jax.random.fold_in(own, 4), (count // 2,), 0, 1 << 20) % (room + 1)
    tallies = tallies.at[giver].add(-shifted).at[sink].add(shifted)
    items = jnp.searchsorted(jnp.cumsum(tallies), jnp.arange(rows * top), side="right").astype(jnp.int32)
    grid = items.reshape(top, rows).T
    grid = grid[jax.random.permutation(jax.random.fold_in(own, 1), rows)]
    rotation = jax.random.randint(jax.random.fold_in(own, 2), (rows, 1), 0, top)
    return jnp.take_along_axis(grid, (jnp.arange(top)[None, :] + rotation) % top, axis=1)


def portions_of(amount, total, reach, lean, full):
    weights = [(1 << 20) // math.isqrt(standing ** lean) + 1 for standing in range(1, amount + 1)]
    largest = reach if full else min(reach, max(-(-total // amount), total * weights[0] // sum(weights)))
    least = 1 if total - largest >= amount - 1 else 0
    given, spare = [largest] + [least] * (amount - 1), total - largest - least * (amount - 1)
    while spare > 0:
        movable = [i for i in range(1, amount) if given[i] < largest] or [i for i in range(1, amount) if given[i] < reach]
        pool, left = sum([weights[i] for i in movable]), spare
        for i in movable:
            more = min(reach - given[i], max(1, left * weights[i] // pool), spare)
            given[i] = given[i] + more
            spare = spare - more
    return np.array(given)


def gaussian(key, dims, scale, reach, split=(), held_as=jnp.bfloat16):
    result = scale * jax.random.normal(key, dims, jnp.float32)
    if split:
        result = result * steps_of(key, dims, split, -0.22, 0.18)
    return jnp.clip(result, -reach, reach).astype(held_as)


def setup_inputs(seed: int = 0) -> dict:
    arg_keys = jax.random.split(jax.random.key(seed), 9)
    tokens = gaussian(arg_keys[0], (TOKENS, D), 1.0, 6.0, ((0, 32),))
    routes_keys = jax.random.split(jax.random.fold_in(arg_keys[1], 1), TOKENS // TOK_DEV)
    routes_turns = jax.random.permutation(jax.random.fold_in(arg_keys[1], 3), TOKENS // TOK_DEV)
    routes = jax.vmap(lambda own, number: routed_block(jax.random.fold_in(arg_keys[1], 2), own, number, TOK_DEV, EXPERTS, 2, CAP, 2))(routes_keys, routes_turns).reshape((TOKENS, 2))
    combine = jnp.clip(jnp.exp(math.log(1.0) - 2.3025851 * jax.random.uniform(arg_keys[2], (TOKENS, 2), jnp.float32) ** steps_of(arg_keys[2], (TOKENS, 2), ((0, 32),), -0.2, 0.2)), 0.1, 1.0)
    w_in = gaussian(arg_keys[3], (D, EXPERTS * FF), D ** -0.5, 0.15625, ((1, 32),))
    w_out = gaussian(arg_keys[4], (EXPERTS * FF, D), FF ** -0.5, 0.078125, ((0, 32),))
    out_grad = gaussian(arg_keys[5], (TOKENS, D), 1.0, 6.0, ((0, 32),))
    head_w = gaussian(arg_keys[6], (D, CLASSES), (D // 9) ** -0.5, 0.5, ((1, 4),))
    labels = with_ends(ranked_ids(arg_keys[7], (IMAGES, LAB), CLASSES, 2), jax.random.fold_in(arg_keys[7], 3), 0, CLASSES - 1).astype(jnp.int32)
    return {"tokens": tokens, "routes": routes, "combine": combine, "w_in": w_in, "w_out": w_out, "out_grad": out_grad, "head_w": head_w, "labels": labels}


beta_rate = 0.99
norm_eps = 1e-06

def gelu_fn(values):
    return jax.nn.gelu(values, approximate=True)

def normalize(pooled):
    center = lax.optimization_barrier(jnp.mean(pooled, axis=1, keepdims=True))
    spread = lax.optimization_barrier(jnp.mean(jnp.square(pooled - center), axis=1, keepdims=True))
    return (pooled - center) * lax.rsqrt(spread + norm_eps)

def weighted_focal(logit_vals, targets, class_weight):
    nll_vals = targets * jax.nn.softplus(-logit_vals) + (1.0 - targets) * jax.nn.softplus(logit_vals)
    return class_weight[None, :] * jnp.square(1.0 - jnp.exp(-nll_vals)) * nll_vals

def expert_pass(xs_rows, grad_rows, w_first, w_second):
    h_pre = jnp.dot(xs_rows, w_first, preferred_element_type=jnp.float32)
    hidden, gelu_back = jax.vjp(gelu_fn, h_pre)
    hidden_bf = hidden.astype(jnp.bfloat16)
    expert_out = jnp.dot(hidden_bf, w_second, preferred_element_type=jnp.float32)
    d_hidden = lax.dot_general(grad_rows, w_second, (((1,), (1,)), ((), ())), preferred_element_type=jnp.float32)
    d_pre = gelu_back(d_hidden)[0].astype(jnp.bfloat16)
    d_second = lax.dot_general(hidden_bf, grad_rows, (((0,), (0,)), ((), ())), preferred_element_type=jnp.float32).astype(jnp.bfloat16)
    d_first = lax.dot_general(xs_rows, d_pre, (((0,), (0,)), ((), ())), preferred_element_type=jnp.float32).astype(jnp.bfloat16)
    d_rows = lax.dot_general(d_pre, w_first, (((1,), (1,)), ((), ())), preferred_element_type=jnp.float32)
    return (expert_out, d_rows, d_first, d_second)

def reference(tokens, routes, combine, w_in, w_out, out_grad, head_w, labels):
    n_devices = N_DP * N_EXPERT
    flat_routes = routes.reshape(n_devices, TOK_DEV * 2)
    route_hits = (flat_routes[:, :, None] == jnp.arange(EXPERTS, dtype=jnp.int32)[None, None, :]).astype(jnp.int32)
    earlier = jnp.cumsum(route_hits, axis=1) - route_hits
    slot_pos = lax.optimization_barrier(jnp.sum(earlier * route_hits, axis=2)).astype(jnp.int32)
    dev_ids = jnp.broadcast_to(jnp.arange(n_devices, dtype=jnp.int32)[:, None], flat_routes.shape)
    tok_pairs = jnp.broadcast_to(tokens.reshape(n_devices, TOK_DEV, 1, D), (n_devices, TOK_DEV, 2, D)).reshape(n_devices, TOK_DEV * 2, D)
    pair_grad = (combine[:, :, None] * out_grad.astype(jnp.float32)[:, None, :]).astype(jnp.bfloat16)
    grad_pairs = pair_grad.reshape(n_devices, TOK_DEV * 2, D)
    x_buf = jnp.zeros((EXPERTS, n_devices, CAP, D), jnp.bfloat16).at[flat_routes, dev_ids, slot_pos].set(tok_pairs)
    g_buf = jnp.zeros((EXPERTS, n_devices, CAP, D), jnp.bfloat16).at[flat_routes, dev_ids, slot_pos].set(grad_pairs)
    w_in_e = w_in.reshape(D, EXPERTS, FF).transpose(1, 0, 2)
    w_out_e = w_out.reshape(EXPERTS, FF, D)

    def one_expert(operands):
        xs_block, grad_block, w_first, w_second = operands
        return expert_pass(xs_block.reshape(n_devices * CAP, D), grad_block.reshape(n_devices * CAP, D), w_first, w_second)
    outs_e, drows_e, dfirst_e, dsecond_e = lax.map(one_expert, (x_buf, g_buf, w_in_e, w_out_e))
    expert_vals = outs_e.reshape(EXPERTS, n_devices, CAP, D)[flat_routes, dev_ids, slot_pos].reshape(TOKENS, 2, D)
    expert_back = drows_e.reshape(EXPERTS, n_devices, CAP, D)[flat_routes, dev_ids, slot_pos].reshape(TOKENS, 2, D)
    mixed_out = (tokens.astype(jnp.float32) + lax.optimization_barrier(jnp.sum(combine[:, :, None] * expert_vals, axis=1))).astype(jnp.bfloat16)
    d_tokens = (out_grad.astype(jnp.float32) + lax.optimization_barrier(jnp.sum(expert_back, axis=1))).astype(jnp.bfloat16)
    d_combine = lax.optimization_barrier(jnp.sum(out_grad.astype(jnp.float32)[:, None, :] * expert_vals, axis=2))
    d_w_in = dfirst_e.transpose(1, 0, 2).reshape(D, EXPERTS * FF)
    d_w_out = dsecond_e.reshape(EXPERTS * FF, D)
    pooled = lax.optimization_barrier(jnp.sum(mixed_out.astype(jnp.float32).reshape(IMAGES, PATCHES, D), axis=1)) / PATCHES
    normed, norm_back = jax.vjp(normalize, pooled)
    normed_bf = normed.astype(jnp.bfloat16)
    logits = jnp.dot(normed_bf, head_w, preferred_element_type=jnp.float32)
    class_ids = jnp.arange(CLASSES, dtype=jnp.int32)
    targets = jnp.any(labels[:, :, None] == class_ids[None, None, :], axis=1).astype(jnp.float32)
    counts = lax.optimization_barrier(jnp.sum(targets, axis=0))
    effective = (1.0 - beta_rate) / (1.0 - jnp.power(beta_rate, counts + 1.0))
    class_weight = effective * CLASSES / jnp.sum(effective)
    focal_terms, focal_back = jax.vjp(lambda logit_vals: weighted_focal(logit_vals, targets, class_weight), logits)
    image_loss = lax.optimization_barrier(jnp.sum(focal_terms, axis=1))
    d_logits = focal_back(jnp.ones_like(focal_terms))[0].astype(jnp.bfloat16)
    d_head = lax.dot_general(normed_bf, d_logits, (((0,), (0,)), ((), ())), preferred_element_type=jnp.float32).astype(jnp.bfloat16)
    d_normed = lax.dot_general(d_logits, head_w, (((1,), (1,)), ((), ())), preferred_element_type=jnp.float32)
    d_pooled = norm_back(d_normed)[0]
    return (mixed_out, d_tokens, d_combine, d_w_in, d_w_out, image_loss, d_pooled, d_head)
```

```python
import jax
import jax.numpy as jnp
from jax import lax
from jax.sharding import PartitionSpec as P

D = 1280
EXPERTS = 32
PATCHES = 256
CLASSES = 17408


beta_rate = 0.99
norm_eps = 1e-06


def gelu_fn(values):
    return jax.nn.gelu(values, approximate=True)


def normalize(pooled):
    center = jnp.mean(pooled, axis=1, keepdims=True)
    spread = jnp.mean(jnp.square(pooled - center), axis=1, keepdims=True)
    return (pooled - center) * lax.rsqrt(spread + norm_eps)


def weighted_focal(logit_vals, targets, class_weight):
    nll_vals = targets * jax.nn.softplus(-logit_vals) + (1.0 - targets) * jax.nn.softplus(
        logit_vals
    )
    return class_weight[None, :] * jnp.square(1.0 - jnp.exp(-nll_vals)) * nll_vals


def swap(messages):
    return lax.all_to_all(messages, ("dp", "expert"), split_axis=0, concat_axis=0, tiled=True)


def pack(rows, n_devices):
    return rows.reshape(n_devices, -1, 128)


def unpack(messages):
    return messages.reshape(-1, D)


def contract_last(left, right):
    return lax.dot_general(left, right, (((1,), (1,)), ((), ())), preferred_element_type=jnp.float32)


def contract_first(left, right):
    return lax.dot_general(left, right, (((0,), (0,)), ((), ())), preferred_element_type=jnp.float32)


def share_out(rows, capacity, share_count):
    rows = rows.reshape(EXPERTS, 1, capacity, D)
    return jnp.broadcast_to(rows, (EXPERTS, share_count, capacity, D)).reshape(-1, D)


def shards(tokens, routes, combine, w_in, w_out, out_grad, head_w, labels):
    dp_size = lax.axis_size("dp")
    ex_size = lax.axis_size("expert")
    n_devices = dp_size * ex_size
    tok_rows = tokens.shape[0]
    capacity = 5 * tok_rows // 64
    share_count = n_devices // EXPERTS
    buffer_rows = EXPERTS * capacity
    ex_index = lax.axis_index("expert")
    dp_index = lax.axis_index("dp")

    flat_routes = routes.reshape(tok_rows * 2)
    route_hits = (flat_routes[:, None] == jnp.arange(EXPERTS, dtype=jnp.int32)[None, :]).astype(
        jnp.int32
    )
    earlier = jnp.cumsum(route_hits, axis=0) - route_hits
    slot_pos = jnp.sum(earlier * route_hits, axis=1)
    slot_index = flat_routes * capacity + slot_pos
    pair_table = (jnp.arange(buffer_rows, dtype=jnp.int32)[:, None] == slot_index[None, :]).astype(
        jnp.bfloat16
    )
    token_table = jnp.sum(pair_table.reshape(buffer_rows, tok_rows, 2), axis=2)
    pair_grad = (
        (combine[:, :, None] * out_grad.astype(jnp.float32)[:, None, :])
        .astype(jnp.bfloat16)
        .reshape(tok_rows * 2, D)
    )
    x_buf = jnp.dot(token_table, tokens, preferred_element_type=jnp.float32).astype(jnp.bfloat16)
    g_buf = jnp.dot(pair_table, pair_grad, preferred_element_type=jnp.float32).astype(jnp.bfloat16)
    x_msg = pack(share_out(x_buf, capacity, share_count), n_devices)
    g_msg = pack(share_out(g_buf, capacity, share_count), n_devices)

    class_cols = head_w.shape[1]
    all_labels = lax.all_gather(labels, "dp", axis=0, tiled=True)
    all_ids = jnp.arange(CLASSES, dtype=jnp.int32)
    counts = jnp.sum(
        jnp.any(all_labels[:, :, None] == all_ids[None, None, :], axis=1).astype(jnp.float32), axis=0
    )
    effective = (1.0 - beta_rate) / (1.0 - jnp.power(beta_rate, counts + 1.0))
    all_weight = effective * CLASSES / jnp.sum(effective)
    class_weight = lax.dynamic_slice_in_dim(all_weight, ex_index * class_cols, class_cols)
    class_ids = ex_index * class_cols + jnp.arange(class_cols, dtype=jnp.int32)
    targets = jnp.any(labels[:, :, None] == class_ids[None, None, :], axis=1).astype(jnp.float32)

    x_in = swap(x_msg)
    x_in, g_msg = lax.optimization_barrier((x_in, g_msg))
    g_in = swap(g_msg)
    xs_rows = unpack(x_in)
    h_pre = jnp.dot(xs_rows, w_in, preferred_element_type=jnp.float32)
    hidden, gelu_back = jax.vjp(gelu_fn, h_pre)
    hidden_bf = hidden.astype(jnp.bfloat16)
    expert_out = jnp.dot(hidden_bf, w_out, preferred_element_type=jnp.float32).astype(jnp.bfloat16)
    out_msg = pack(expert_out, n_devices)
    out_msg, g_in = lax.optimization_barrier((out_msg, g_in))
    back_out = swap(out_msg)

    grad_rows = unpack(g_in)
    d_hidden = contract_last(grad_rows, w_out)
    d_pre = gelu_back(d_hidden)[0].astype(jnp.bfloat16)
    d_rows = contract_last(d_pre, w_in).astype(jnp.bfloat16)
    rows_msg = pack(d_rows, n_devices)
    rows_msg, d_pre, hidden_bf = lax.optimization_barrier((rows_msg, d_pre, hidden_bf))
    back_rows = swap(rows_msg)
    d_w_out = contract_first(hidden_bf, grad_rows).astype(jnp.bfloat16)
    d_w_in = contract_first(xs_rows, d_pre).astype(jnp.bfloat16)

    def collect(messages):
        rows = unpack(messages).reshape(EXPERTS, share_count, capacity, D)
        rows = jnp.sum(rows.astype(jnp.float32), axis=1).reshape(buffer_rows, D)
        return contract_first(pair_table, rows.astype(jnp.bfloat16)).reshape(tok_rows, 2, D) if (
            share_count == 1
        ) else jnp.take(rows, slot_index, axis=0).reshape(tok_rows, 2, D)

    expert_vals = collect(back_out)
    mixed_out = (
        tokens.astype(jnp.float32) + jnp.sum(combine[:, :, None] * expert_vals, axis=1)
    ).astype(jnp.bfloat16)
    d_combine = jnp.sum(out_grad.astype(jnp.float32)[:, None, :] * expert_vals, axis=2)

    images = labels.shape[0]
    token_image = (ex_index * tok_rows + jnp.arange(tok_rows, dtype=jnp.int32)) // PATCHES
    mixed_f32 = mixed_out.astype(jnp.float32)
    pooled_part = jnp.stack(
        [
            jnp.sum(jnp.where((token_image == image)[:, None], mixed_f32, 0.0), axis=0)
            for image in range(images)
        ]
    )
    pooled = lax.psum(pooled_part, "expert") / PATCHES
    normed, norm_back = jax.vjp(normalize, pooled)
    normed_bf = normed.astype(jnp.bfloat16)
    logits = jnp.dot(normed_bf, head_w, preferred_element_type=jnp.float32)
    focal_terms, focal_back = jax.vjp(
        lambda logit_vals: weighted_focal(logit_vals, targets, class_weight), logits
    )
    d_logits = focal_back(jnp.ones_like(focal_terms))[0].astype(jnp.bfloat16)
    pairs = lax.all_gather(
        jnp.concatenate([normed_bf, d_logits], axis=1), "dp", axis=0, tiled=True
    )
    normed_part = contract_last(d_logits, head_w)
    d_normed, image_loss = lax.psum((normed_part, jnp.sum(focal_terms, axis=1)), "expert")
    d_pooled = norm_back(d_normed)[0]
    head_rows = D // dp_size
    own_normed = lax.dynamic_slice_in_dim(pairs[:, :D], dp_index * head_rows, head_rows, axis=1)
    d_head = contract_first(own_normed, pairs[:, D:]).astype(jnp.bfloat16)

    expert_back = collect(back_rows)
    d_tokens = (out_grad.astype(jnp.float32) + jnp.sum(expert_back, axis=1)).astype(jnp.bfloat16)
    return (mixed_out, d_tokens, d_combine, d_w_in, d_w_out, image_loss, d_pooled, d_head)


def solution(mesh):
    in_specs = (
        P(("dp", "expert"), None),
        P(("dp", "expert"), None),
        P(("dp", "expert"), None),
        P(None, ("dp", "expert")),
        P(("dp", "expert"), None),
        P(("dp", "expert"), None),
        P(None, "expert"),
        P("dp", None),
    )
    out_specs = (
        P(("dp", "expert"), None),
        P(("dp", "expert"), None),
        P(("dp", "expert"), None),
        P(None, ("dp", "expert")),
        P(("dp", "expert"), None),
        P("dp"),
        P("dp", None),
        P("dp", "expert"),
    )
    return jax.shard_map(shards, mesh=mesh, in_specs=in_specs, out_specs=out_specs, check_vma=False)
```

```python
import functools

import jax
import jax.numpy as jnp
from jax import lax
from jax.experimental import pallas as pl
from jax.experimental.pallas import tpu as pltpu
from jax.sharding import PartitionSpec as P

D = 1280
EXPERTS = 32
PATCHES = 256
CLASSES = 17408


beta_rate = 0.99
norm_eps = 1e-06


def gelu_fn(values):
    return jax.nn.gelu(values, approximate=True)


def normalize(pooled):
    center = jnp.mean(pooled, axis=1, keepdims=True)
    spread = jnp.mean(jnp.square(pooled - center), axis=1, keepdims=True)
    return (pooled - center) * lax.rsqrt(spread + norm_eps)


def weighted_focal(logit_vals, targets, class_weight):
    nll_vals = targets * jax.nn.softplus(-logit_vals) + (1.0 - targets) * jax.nn.softplus(
        logit_vals
    )
    return class_weight[None, :] * jnp.square(1.0 - jnp.exp(-nll_vals)) * nll_vals


def swap(messages):
    return lax.all_to_all(messages, ("dp", "expert"), split_axis=0, concat_axis=0, tiled=True)


def pack(rows, n_devices):
    return rows.reshape(n_devices, -1, 128)


def unpack(messages):
    return messages.reshape(-1, D)


def contract_last(left, right):
    return lax.dot_general(left, right, (((1,), (1,)), ((), ())), preferred_element_type=jnp.float32)


def contract_first(left, right):
    return lax.dot_general(left, right, (((0,), (0,)), ((), ())), preferred_element_type=jnp.float32)


def share_out(rows, capacity, share_count):
    rows = rows.reshape(EXPERTS, 1, capacity, D)
    return jnp.broadcast_to(rows, (EXPERTS, share_count, capacity, D)).reshape(-1, D)


def gather_kernel(axes, *refs):
    count = len(axes)
    sources, results = refs[:count], refs[count : 2 * count]
    send_sems, recv_sems = refs[2 * count : 3 * count], refs[3 * count :]
    partners = [
        (axis, shift, lax.rem(lax.axis_index(axis) + shift, lax.axis_size(axis)))
        for axis in axes
        for shift in range(1, lax.axis_size(axis))
    ]
    barrier = pltpu.get_barrier_semaphore()
    for axis, _, peer in partners:
        pl.semaphore_signal(
            barrier, inc=1, device_id={axis: peer}, device_id_type=pl.DeviceIdType.MESH
        )
    pl.semaphore_wait(barrier, len(partners))
    copies = []
    for axis, shift, peer in partners:
        item = axes.index(axis)
        copy = pltpu.make_async_remote_copy(
            src_ref=sources[item],
            dst_ref=results[item].at[lax.axis_index(axis)],
            send_sem=send_sems[item].at[shift],
            recv_sem=recv_sems[item].at[shift],
            device_id={axis: peer},
            device_id_type=pl.DeviceIdType.MESH,
        )
        copy.start()
        copies.append(copy)
    for axis, source, result in zip(axes, sources, results):
        result[lax.axis_index(axis)] = source[...]
    for copy in copies:
        copy.wait()


def gather(arrays, axes, collective_id):
    sizes = [lax.axis_size(axis) for axis in axes]
    moved = sum(size * array.size * 4 for size, array in zip(sizes, arrays))
    return pl.pallas_call(
        functools.partial(gather_kernel, axes),
        out_shape=[
            jax.ShapeDtypeStruct((size,) + array.shape, array.dtype)
            for size, array in zip(sizes, arrays)
        ],
        in_specs=[pl.BlockSpec(memory_space=pltpu.VMEM)] * len(axes),
        out_specs=[pl.BlockSpec(memory_space=pltpu.VMEM)] * len(axes),
        scratch_shapes=[pltpu.SemaphoreType.DMA((size,)) for size in sizes] * 2,
        compiler_params=pltpu.CompilerParams(
            collective_id=collective_id,
            has_side_effects=True,
            vmem_limit_bytes=8 * 1024 * 1024,
        ),
        cost_estimate=pl.CostEstimate(flops=0, bytes_accessed=moved, transcendentals=0),
    )(*arrays)


def shards(tokens, routes, combine, w_in, w_out, out_grad, head_w, labels):
    dp_size = lax.axis_size("dp")
    ex_size = lax.axis_size("expert")
    n_devices = dp_size * ex_size
    tok_rows = tokens.shape[0]
    capacity = 5 * tok_rows // 64
    share_count = n_devices // EXPERTS
    buffer_rows = EXPERTS * capacity
    ex_index = lax.axis_index("expert")
    dp_index = lax.axis_index("dp")

    flat_routes = routes.reshape(tok_rows * 2)
    route_hits = (flat_routes[:, None] == jnp.arange(EXPERTS, dtype=jnp.int32)[None, :]).astype(
        jnp.int32
    )
    earlier = jnp.cumsum(route_hits, axis=0) - route_hits
    slot_pos = jnp.sum(earlier * route_hits, axis=1)
    slot_index = flat_routes * capacity + slot_pos
    pair_table = (jnp.arange(buffer_rows, dtype=jnp.int32)[:, None] == slot_index[None, :]).astype(
        jnp.bfloat16
    )
    token_table = jnp.sum(pair_table.reshape(buffer_rows, tok_rows, 2), axis=2)
    pair_grad = (
        (combine[:, :, None] * out_grad.astype(jnp.float32)[:, None, :])
        .astype(jnp.bfloat16)
        .reshape(tok_rows * 2, D)
    )
    x_buf = jnp.dot(token_table, tokens, preferred_element_type=jnp.float32).astype(jnp.bfloat16)
    g_buf = jnp.dot(pair_table, pair_grad, preferred_element_type=jnp.float32).astype(jnp.bfloat16)
    x_msg = pack(share_out(x_buf, capacity, share_count), n_devices)
    g_msg = pack(share_out(g_buf, capacity, share_count), n_devices)

    class_cols = head_w.shape[1]
    label_rows, label_count = labels.shape
    label_block = jnp.pad(labels, ((0, -label_rows % 8), (0, 128 - label_count)))
    label_block, g_msg = lax.optimization_barrier((label_block, g_msg))
    (all_labels,) = gather([label_block], ("dp",), 0)
    all_labels = all_labels[:, :label_rows, :label_count].reshape(-1, label_count)
    all_ids = jnp.arange(CLASSES, dtype=jnp.int32)
    counts = jnp.sum(
        jnp.any(all_labels[:, :, None] == all_ids[None, None, :], axis=1).astype(jnp.float32), axis=0
    )
    effective = (1.0 - beta_rate) / (1.0 - jnp.power(beta_rate, counts + 1.0))
    all_weight = effective * CLASSES / jnp.sum(effective)
    class_weight = lax.dynamic_slice_in_dim(all_weight, ex_index * class_cols, class_cols)
    class_ids = ex_index * class_cols + jnp.arange(class_cols, dtype=jnp.int32)
    targets = jnp.any(labels[:, :, None] == class_ids[None, None, :], axis=1).astype(jnp.float32)

    x_in = swap(x_msg)
    x_in, g_msg = lax.optimization_barrier((x_in, g_msg))
    g_in = swap(g_msg)
    xs_rows = unpack(x_in)
    h_pre = jnp.dot(xs_rows, w_in, preferred_element_type=jnp.float32)
    hidden, gelu_back = jax.vjp(gelu_fn, h_pre)
    hidden_bf = hidden.astype(jnp.bfloat16)
    expert_out = jnp.dot(hidden_bf, w_out, preferred_element_type=jnp.float32).astype(jnp.bfloat16)
    out_msg = pack(expert_out, n_devices)
    out_msg, g_in = lax.optimization_barrier((out_msg, g_in))
    back_out = swap(out_msg)

    grad_rows = unpack(g_in)
    d_hidden = contract_last(grad_rows, w_out)
    d_pre = gelu_back(d_hidden)[0].astype(jnp.bfloat16)
    d_rows = contract_last(d_pre, w_in).astype(jnp.bfloat16)
    rows_msg = pack(d_rows, n_devices)
    rows_msg, d_pre, hidden_bf = lax.optimization_barrier((rows_msg, d_pre, hidden_bf))
    back_rows = swap(rows_msg)
    d_w_out = contract_first(hidden_bf, grad_rows).astype(jnp.bfloat16)
    d_w_in = contract_first(xs_rows, d_pre).astype(jnp.bfloat16)

    def collect(messages):
        rows = unpack(messages).reshape(EXPERTS, share_count, capacity, D)
        rows = jnp.sum(rows.astype(jnp.float32), axis=1).reshape(buffer_rows, D)
        return contract_first(pair_table, rows.astype(jnp.bfloat16)).reshape(tok_rows, 2, D) if (
            share_count == 1
        ) else jnp.take(rows, slot_index, axis=0).reshape(tok_rows, 2, D)

    expert_vals = collect(back_out)
    mixed_out = (
        tokens.astype(jnp.float32) + jnp.sum(combine[:, :, None] * expert_vals, axis=1)
    ).astype(jnp.bfloat16)
    d_combine = jnp.sum(out_grad.astype(jnp.float32)[:, None, :] * expert_vals, axis=2)

    images = labels.shape[0]
    token_image = (ex_index * tok_rows + jnp.arange(tok_rows, dtype=jnp.int32)) // PATCHES
    mixed_f32 = mixed_out.astype(jnp.float32)
    pooled_part = jnp.stack(
        [
            jnp.sum(jnp.where((token_image == image)[:, None], mixed_f32, 0.0), axis=0)
            for image in range(images)
        ]
    )
    (pooled_parts,) = gather([pooled_part], ("expert",), 1)
    pooled = jnp.sum(pooled_parts, axis=0) / PATCHES
    normed, norm_back = jax.vjp(normalize, pooled)
    normed_bf = normed.astype(jnp.bfloat16)
    logits = jnp.dot(normed_bf, head_w, preferred_element_type=jnp.float32)
    focal_terms, focal_back = jax.vjp(
        lambda logit_vals: weighted_focal(logit_vals, targets, class_weight), logits
    )
    d_logits = focal_back(jnp.ones_like(focal_terms))[0].astype(jnp.bfloat16)
    normed_part = contract_last(d_logits, head_w)
    loss_part = jnp.broadcast_to(jnp.sum(focal_terms, axis=1)[:, None], (images, 128))
    pairs, parts = gather(
        [
            jnp.concatenate([normed_bf, d_logits], axis=1).astype(jnp.float32),
            jnp.concatenate([normed_part, loss_part], axis=1),
        ],
        ("dp", "expert"),
        2,
    )
    pairs = pairs.reshape(-1, D + class_cols).astype(jnp.bfloat16)
    parts = jnp.sum(parts, axis=0)
    d_normed, image_loss = parts[:, :D], parts[:, D]
    d_pooled = norm_back(d_normed)[0]
    head_rows = D // dp_size
    own_normed = lax.dynamic_slice_in_dim(pairs[:, :D], dp_index * head_rows, head_rows, axis=1)
    d_head = contract_first(own_normed, pairs[:, D:]).astype(jnp.bfloat16)

    expert_back = collect(back_rows)
    d_tokens = (out_grad.astype(jnp.float32) + jnp.sum(expert_back, axis=1)).astype(jnp.bfloat16)
    return (mixed_out, d_tokens, d_combine, d_w_in, d_w_out, image_loss, d_pooled, d_head)


def solution(mesh):
    in_specs = (
        P(("dp", "expert"), None),
        P(("dp", "expert"), None),
        P(("dp", "expert"), None),
        P(None, ("dp", "expert")),
        P(("dp", "expert"), None),
        P(("dp", "expert"), None),
        P(None, "expert"),
        P("dp", None),
    )
    out_specs = (
        P(("dp", "expert"), None),
        P(("dp", "expert"), None),
        P(("dp", "expert"), None),
        P(None, ("dp", "expert")),
        P(("dp", "expert"), None),
        P("dp"),
        P("dp", None),
        P("dp", "expert"),
    )
    return jax.shard_map(shards, mesh=mesh, in_specs=in_specs, out_specs=out_specs, check_vma=False)
```

```python
import functools

import jax
import jax.numpy as jnp
from jax import lax
from jax.experimental import pallas as pl
from jax.experimental.pallas import tpu as pltpu
from jax.sharding import PartitionSpec as P

D = 1280
EXPERTS = 32
PATCHES = 256
CLASSES = 17408


beta_rate = 0.99
norm_eps = 1e-06


def gelu_fn(values):
    return jax.nn.gelu(values, approximate=True)


def normalize(pooled):
    center = jnp.mean(pooled, axis=1, keepdims=True)
    spread = jnp.mean(jnp.square(pooled - center), axis=1, keepdims=True)
    return (pooled - center) * lax.rsqrt(spread + norm_eps)


def weighted_focal(logit_vals, targets, class_weight):
    nll_vals = targets * jax.nn.softplus(-logit_vals) + (1.0 - targets) * jax.nn.softplus(
        logit_vals
    )
    return class_weight[None, :] * jnp.square(1.0 - jnp.exp(-nll_vals)) * nll_vals


def swap(messages):
    return lax.all_to_all(messages, ("dp", "expert"), split_axis=0, concat_axis=0, tiled=True)


def pack(rows, n_devices):
    return rows.reshape(n_devices, -1, 128)


def unpack(messages):
    return messages.reshape(-1, D)


def contract_last(left, right):
    return lax.dot_general(left, right, (((1,), (1,)), ((), ())), preferred_element_type=jnp.float32)


def contract_first(left, right):
    return lax.dot_general(left, right, (((0,), (0,)), ((), ())), preferred_element_type=jnp.float32)


def share_out(rows, capacity, share_count):
    rows = rows.reshape(EXPERTS, 1, capacity, D)
    return jnp.broadcast_to(rows, (EXPERTS, share_count, capacity, D)).reshape(-1, D)


def gather_kernel(axes, *refs):
    count = len(axes)
    sources, results = refs[:count], refs[count : 2 * count]
    send_sems, recv_sems = refs[2 * count : 3 * count], refs[3 * count :]
    partners = [
        (axis, shift, lax.rem(lax.axis_index(axis) + shift, lax.axis_size(axis)))
        for axis in axes
        for shift in range(1, lax.axis_size(axis))
    ]
    barrier = pltpu.get_barrier_semaphore()
    for axis, _, peer in partners:
        pl.semaphore_signal(
            barrier, inc=1, device_id={axis: peer}, device_id_type=pl.DeviceIdType.MESH
        )
    pl.semaphore_wait(barrier, len(partners))
    copies = []
    for axis, shift, peer in partners:
        item = axes.index(axis)
        copy = pltpu.make_async_remote_copy(
            src_ref=sources[item],
            dst_ref=results[item].at[lax.axis_index(axis)],
            send_sem=send_sems[item].at[shift],
            recv_sem=recv_sems[item].at[shift],
            device_id={axis: peer},
            device_id_type=pl.DeviceIdType.MESH,
        )
        copy.start()
        copies.append(copy)
    for axis, source, result in zip(axes, sources, results):
        result[lax.axis_index(axis)] = source[...]
    for copy in copies:
        copy.wait()


def gather(arrays, axes, collective_id):
    sizes = [lax.axis_size(axis) for axis in axes]
    moved = sum(size * array.size * 4 for size, array in zip(sizes, arrays))
    return pl.pallas_call(
        functools.partial(gather_kernel, axes),
        out_shape=[
            jax.ShapeDtypeStruct((size,) + array.shape, array.dtype)
            for size, array in zip(sizes, arrays)
        ],
        in_specs=[pl.BlockSpec(memory_space=pltpu.VMEM)] * len(axes),
        out_specs=[pl.BlockSpec(memory_space=pltpu.VMEM)] * len(axes),
        scratch_shapes=[pltpu.SemaphoreType.DMA((size,)) for size in sizes] * 2,
        compiler_params=pltpu.CompilerParams(
            collective_id=collective_id,
            has_side_effects=True,
            vmem_limit_bytes=8 * 1024 * 1024,
        ),
        cost_estimate=pl.CostEstimate(flops=0, bytes_accessed=moved, transcendentals=0),
    )(*arrays)


def shards(tokens, routes, combine, w_in, w_out, out_grad, head_w, labels):
    dp_size = lax.axis_size("dp")
    ex_size = lax.axis_size("expert")
    n_devices = dp_size * ex_size
    tok_rows = tokens.shape[0]
    capacity = 5 * tok_rows // 64
    share_count = n_devices // EXPERTS
    buffer_rows = EXPERTS * capacity
    ex_index = lax.axis_index("expert")
    dp_index = lax.axis_index("dp")

    flat_routes = routes.reshape(tok_rows * 2)
    route_hits = (flat_routes[:, None] == jnp.arange(EXPERTS, dtype=jnp.int32)[None, :]).astype(
        jnp.int32
    )
    earlier = jnp.cumsum(route_hits, axis=0) - route_hits
    slot_pos = jnp.sum(earlier * route_hits, axis=1)
    slot_index = flat_routes * capacity + slot_pos
    pair_table = (jnp.arange(buffer_rows, dtype=jnp.int32)[:, None] == slot_index[None, :]).astype(
        jnp.bfloat16
    )
    token_table = jnp.sum(pair_table.reshape(buffer_rows, tok_rows, 2), axis=2)
    pair_grad = (
        (combine[:, :, None] * out_grad.astype(jnp.float32)[:, None, :])
        .astype(jnp.bfloat16)
        .reshape(tok_rows * 2, D)
    )
    x_buf = jnp.dot(token_table, tokens, preferred_element_type=jnp.float32).astype(jnp.bfloat16)
    g_buf = jnp.dot(pair_table, pair_grad, preferred_element_type=jnp.float32).astype(jnp.bfloat16)
    x_msg = pack(share_out(x_buf, capacity, share_count), n_devices)
    g_msg = pack(share_out(g_buf, capacity, share_count), n_devices)

    class_cols = head_w.shape[1]
    label_rows, label_count = labels.shape
    label_block = jnp.pad(labels, ((0, -label_rows % 8), (0, 128 - label_count)))
    x_in = swap(x_msg)
    x_in, g_msg = lax.optimization_barrier((x_in, g_msg))
    g_in = swap(g_msg)
    xs_rows = unpack(x_in)
    h_pre = jnp.dot(xs_rows, w_in, preferred_element_type=jnp.float32)
    hidden, gelu_back = jax.vjp(gelu_fn, h_pre)
    hidden_bf = hidden.astype(jnp.bfloat16)
    expert_out = jnp.dot(hidden_bf, w_out, preferred_element_type=jnp.float32).astype(jnp.bfloat16)
    out_msg = pack(expert_out, n_devices)
    out_msg, g_in = lax.optimization_barrier((out_msg, g_in))
    back_out = swap(out_msg)

    grad_rows = unpack(g_in)
    d_hidden = contract_last(grad_rows, w_out)
    d_pre = gelu_back(d_hidden)[0].astype(jnp.bfloat16)
    d_rows = contract_last(d_pre, w_in).astype(jnp.bfloat16)
    rows_msg = pack(d_rows, n_devices)
    rows_msg, d_pre, hidden_bf = lax.optimization_barrier((rows_msg, d_pre, hidden_bf))
    back_rows = swap(rows_msg)
    d_w_out = contract_first(hidden_bf, grad_rows).astype(jnp.bfloat16)
    d_w_in = contract_first(xs_rows, d_pre).astype(jnp.bfloat16)

    def collect(messages):
        rows = unpack(messages).reshape(EXPERTS, share_count, capacity, D)
        rows = jnp.sum(rows.astype(jnp.float32), axis=1).reshape(buffer_rows, D)
        return contract_first(pair_table, rows.astype(jnp.bfloat16)).reshape(tok_rows, 2, D) if (
            share_count == 1
        ) else jnp.take(rows, slot_index, axis=0).reshape(tok_rows, 2, D)

    expert_vals = collect(back_out)
    mixed_out = (
        tokens.astype(jnp.float32) + jnp.sum(combine[:, :, None] * expert_vals, axis=1)
    ).astype(jnp.bfloat16)
    d_combine = jnp.sum(out_grad.astype(jnp.float32)[:, None, :] * expert_vals, axis=2)

    images = labels.shape[0]
    token_image = (ex_index * tok_rows + jnp.arange(tok_rows, dtype=jnp.int32)) // PATCHES
    mixed_f32 = mixed_out.astype(jnp.float32)
    pooled_part = jnp.stack(
        [
            jnp.sum(jnp.where((token_image == image)[:, None], mixed_f32, 0.0), axis=0)
            for image in range(images)
        ]
    )
    pooled_part, back_rows = lax.optimization_barrier((pooled_part, back_rows))
    all_labels, pooled_parts = gather([label_block, pooled_part], ("dp", "expert"), 1)
    all_labels = all_labels[:, :label_rows, :label_count].reshape(-1, label_count)
    all_ids = jnp.arange(CLASSES, dtype=jnp.int32)
    counts = jnp.sum(
        jnp.any(all_labels[:, :, None] == all_ids[None, None, :], axis=1).astype(jnp.float32), axis=0
    )
    effective = (1.0 - beta_rate) / (1.0 - jnp.power(beta_rate, counts + 1.0))
    all_weight = effective * CLASSES / jnp.sum(effective)
    class_weight = lax.dynamic_slice_in_dim(all_weight, ex_index * class_cols, class_cols)
    class_ids = ex_index * class_cols + jnp.arange(class_cols, dtype=jnp.int32)
    targets = jnp.any(labels[:, :, None] == class_ids[None, None, :], axis=1).astype(jnp.float32)

    pooled = jnp.sum(pooled_parts, axis=0) / PATCHES
    normed, norm_back = jax.vjp(normalize, pooled)
    normed_bf = normed.astype(jnp.bfloat16)
    logits = jnp.dot(normed_bf, head_w, preferred_element_type=jnp.float32)
    focal_terms, focal_back = jax.vjp(
        lambda logit_vals: weighted_focal(logit_vals, targets, class_weight), logits
    )
    d_logits = focal_back(jnp.ones_like(focal_terms))[0].astype(jnp.bfloat16)
    normed_part = contract_last(d_logits, head_w)
    loss_part = jnp.broadcast_to(jnp.sum(focal_terms, axis=1)[:, None], (images, 128))
    pairs, parts = gather(
        [
            jnp.concatenate([normed_bf, d_logits], axis=1).astype(jnp.float32),
            jnp.concatenate([normed_part, loss_part], axis=1),
        ],
        ("dp", "expert"),
        2,
    )
    pairs = pairs.reshape(-1, D + class_cols).astype(jnp.bfloat16)
    parts = jnp.sum(parts, axis=0)
    d_normed, image_loss = parts[:, :D], parts[:, D]
    d_pooled = norm_back(d_normed)[0]
    head_rows = D // dp_size
    own_normed = lax.dynamic_slice_in_dim(pairs[:, :D], dp_index * head_rows, head_rows, axis=1)
    d_head = contract_first(own_normed, pairs[:, D:]).astype(jnp.bfloat16)

    expert_back = collect(back_rows)
    d_tokens = (out_grad.astype(jnp.float32) + jnp.sum(expert_back, axis=1)).astype(jnp.bfloat16)
    return (mixed_out, d_tokens, d_combine, d_w_in, d_w_out, image_loss, d_pooled, d_head)


def solution(mesh):
    in_specs = (
        P(("dp", "expert"), None),
        P(("dp", "expert"), None),
        P(("dp", "expert"), None),
        P(None, ("dp", "expert")),
        P(("dp", "expert"), None),
        P(("dp", "expert"), None),
        P(None, "expert"),
        P("dp", None),
    )
    out_specs = (
        P(("dp", "expert"), None),
        P(("dp", "expert"), None),
        P(("dp", "expert"), None),
        P(None, ("dp", "expert")),
        P(("dp", "expert"), None),
        P("dp"),
        P("dp", None),
        P("dp", "expert"),
    )
    return jax.shard_map(shards, mesh=mesh, in_specs=in_specs, out_specs=out_specs, check_vma=False)
```
